32 devices in a mesh: parts: 2 (over x), dom: 16 (over z, y, core).
Axes of the slice: x: 2, y: 2, z: 4, core: 2. Of those that a mesh axis runs over, the one named last changes fastest.
Arguments:
- nodes: bfloat16 [8192, 512], P(('parts', 'dom')), parts along dimension 0, may hold values from -6 to 6
- node_count: int32 [32], P(('parts', 'dom')), parts along dimension 0, may hold values from 64 to 256, as said below
- edge_src: int32 [32768], P(('parts', 'dom')), parts along dimension 0, may hold values from 0 to 383, as said below
- edge_dst: int32 [32768], P(('parts', 'dom')), parts along dimension 0, may hold values from 0 to 255, as said below
- edge_count: int32 [32], P(('parts', 'dom')), parts along dimension 0, may hold values from 256 to 1024, as said below
- send_list: int32 [32, 8, 16], P(('parts', 'dom')), parts along dimension 0, may hold values from 0 to 255, as said below
- assign: int32 [8192], P(('parts', 'dom')), parts along dimension 0, may hold values from 0 to 63, as said below
- w_in: bfloat16 [1024, 1024], replicated, may hold values from -0.1875 to 0.1875
- b_in: float32 [1024], replicated, may hold values from -3 to 3
- w_out: bfloat16 [1024, 512], replicated, may hold values from -0.1875 to 0.1875
- w_back: bfloat16 [512, 512], replicated, may hold values from -0.25 to 0.25
- grad_out: bfloat16 [8192, 512], P(('parts', 'dom')), parts along dimension 0, may hold values from -6 to 6
Outputs:
- fields: bfloat16 [8192, 512], P(('parts', 'dom')), parts along dimension 0
- grad_nodes: bfloat16 [8192, 512], P(('parts', 'dom')), parts along dimension 0
- grad_w_in: float32 [2048, 1024], P(('parts', 'dom')), parts along dimension 0
- grad_b_in: float32 [2048], P(('parts', 'dom')), parts along dimension 0
- grad_w_out: float32 [2048, 512], P(('parts', 'dom')), parts along dimension 0
- grad_w_back: float32 [1024, 512], P(('parts', 'dom')), parts along dimension 0
The draws below stay inside these ranges and needn't reach their ends.
There are 2 independent parts, one for each index of `parts`. The reference program is written for one: setup_inputs(seed, part) draws one part's arguments, and reference() takes and returns one part's arrays. A program takes and returns all parts, laid end to end along the dimension named above; an argument that names none is the same for every part. Nothing has to cross between parts.
Inputs may be any that keep to these rules, and one draw needn't show every extreme that they name: `node_count`: one partition is full in every draw. `edge_count`: one partition is full in every draw. `edge_dst`: below the node count of the edge's partition. `edge_src`: a value under 256 is a row of the edge's own partition below its node count; a larger one is 256 + 16 * k + s, slot s of the rows that the partition's neighbour in direction k sends it, and that neighbour lies on the grid. send_list[j, k, s] is below the node count of partition j. `assign`: a fine node of partition p is assigned a coarse node of (p - 1) * 4 to (p + 2) * 4 - 1, taken modulo 64.
All inputs are finite; a program needn't handle non-finite values.
Results may differ from the reference program's by a relative error of at most 0.008.
Values may be sent and summed in bfloat16 or wider, within the bound.
A program may use at most 64 MiB of HBM per device.

```python
import jax
import jax.numpy as jnp
from jax import lax

D = 512
HID = 1024
NODE_DEV = 256
EDGE_DEV = 1024
SLOT = 16
NEIGHBOURS = 8
GRID_Y = 8
PARTITIONS = 16
CO_DEV = 4
NODES = 4096
EDGES = 16384
COARSE = 64


def partition_counts(key, salt, top):
    base = jax.random.randint(jax.random.fold_in(key, salt), (PARTITIONS,), top // 4, top + 1)
    full = jax.random.randint(jax.random.fold_in(key, salt + 1), (), 0, PARTITIONS)
    counts = jnp.where(jnp.arange(PARTITIONS) == full, top, base).astype(jnp.int32)
    return (counts, full)


def draw_node_count(key, part):
    counts, full = partition_counts(key, 101, NODE_DEV)
    return counts


def draw_edge_count(key, part):
    counts, full = partition_counts(key, 201, EDGE_DEV)
    return counts


def draw_edge_dst(key, part):
    counts, full = partition_counts(key, 101, NODE_DEV)
    key = jax.random.fold_in(key, 5)
    edge_ids = jnp.arange(EDGES, dtype=jnp.int32)
    owner = edge_ids // EDGE_DEV
    raw = jax.random.randint(key, (EDGES,), 0, 1 << 20)
    rows = raw % counts[owner]
    return jnp.where(edge_ids == full * EDGE_DEV, NODE_DEV - 1, rows).astype(jnp.int32)


def draw_edge_src(key, part):
    counts, full = partition_counts(key, 101, NODE_DEV)
    key = jax.random.fold_in(key, 6)
    edge_ids = jnp.arange(EDGES, dtype=jnp.int32)
    owner = edge_ids // EDGE_DEV
    grid_row = owner // GRID_Y
    grid_col = owner % GRID_Y
    shift_rows = jnp.array([-1, -1, -1, 0, 0, 1, 1, 1], dtype=jnp.int32)
    shift_cols = jnp.array([-1, 0, 1, -1, 1, -1, 0, 1], dtype=jnp.int32)
    choose = jax.random.randint(jax.random.fold_in(key, 1), (EDGES,), 0, 6)
    local_rows = jax.random.randint(jax.random.fold_in(key, 2), (EDGES,), 0, 1 << 20) % counts[owner]
    direction = jax.random.randint(jax.random.fold_in(key, 3), (EDGES,), 0, NEIGHBOURS)
    slot_index = jax.random.randint(jax.random.fold_in(key, 4), (EDGES,), 0, SLOT)
    target_row = grid_row + shift_rows[direction]
    target_col = grid_col + shift_cols[direction]
    inside = (target_row >= 0) & (target_row < PARTITIONS // GRID_Y) & (target_col >= 0) & (target_col < GRID_Y)
    halo_rows = NODE_DEV + direction * SLOT + slot_index
    return jnp.where((choose == 0) & inside, halo_rows, local_rows).astype(jnp.int32)


def draw_send_list(key, part):
    counts, full = partition_counts(key, 101, NODE_DEV)
    key = jax.random.fold_in(key, 7)
    raw = jax.random.randint(key, (PARTITIONS, NEIGHBOURS, SLOT), 0, 1 << 20)
    rows = raw % counts[:, None, None]
    marked = (jnp.arange(PARTITIONS)[:, None, None] == full) & (jnp.arange(NEIGHBOURS)[None, :, None] == 0) & (jnp.arange(SLOT)[None, None, :] == 0)
    return jnp.where(marked, NODE_DEV - 1, rows).astype(jnp.int32)


def draw_assign(key, part):
    key = jax.random.fold_in(key, 8)
    owner = jnp.arange(NODES, dtype=jnp.int32) // NODE_DEV
    within = jax.random.randint(key, (NODES,), 0, 3 * CO_DEV)
    raw = (owner * CO_DEV + within - CO_DEV) % COARSE
    empty = jax.random.randint(jax.random.fold_in(key, 1), (), 1, COARSE - 1)
    moved = jnp.where(within < 3 * CO_DEV - 1, within + 1, within - 1)
    within = jnp.where(raw == empty, moved, within)
    return ((owner * CO_DEV + within - CO_DEV) % COARSE).astype(jnp.int32)


def steps_of(rng, shape, shards, least, top_value):
    loudness, own = 1.0, jax.random.fold_in(rng, 6)
    for dim, parts in shards:
        draws = jnp.exp(jax.random.uniform(jax.random.fold_in(own, dim), (parts,), jnp.float32, least / len(shards), top_value / len(shards)))
        loudness = loudness * jnp.repeat(draws, shape[dim] // parts).reshape([-1 if axis == dim else 1 for axis in range(len(shape))])
    return loudness


def bell_draw(own_key, dims, width, reach, cuts=(), kind=jnp.bfloat16):
    values = width * jax.random.normal(own_key, dims, jnp.float32)
    if cuts:
        values = values * steps_of(own_key, dims, cuts, -0.22, 0.18)
    return jnp.clip(values, -reach, reach).astype(kind)


def setup_inputs(seed: int = 0, part: int = 0) -> dict:
    keys = jax.random.split(jax.random.key(seed), 13)
    own_keys = jax.random.split(jax.random.fold_in(keys[12], part), 13)
    nodes = bell_draw(own_keys[0], (NODES, D), 1.0, 6.0, ((0, 16),))
    node_count = draw_node_count(jax.random.fold_in(jax.random.fold_in(keys[12], part), 71), part)
    edge_src = draw_edge_src(jax.random.fold_in(jax.random.fold_in(keys[12], part), 71), part)
    edge_dst = draw_edge_dst(jax.random.fold_in(jax.random.fold_in(keys[12], part), 71), part)
    edge_count = draw_edge_count(jax.random.fold_in(jax.random.fold_in(keys[12], part), 71), part)
    send_list = draw_send_list(jax.random.fold_in(jax.random.fold_in(keys[12], part), 71), part)
    assign = draw_assign(jax.random.fold_in(jax.random.fold_in(keys[12], part), 71), part)
    w_in = bell_draw(keys[7], (2 * D, HID), (2 * D) ** -0.5, 0.1875)
    b_in = bell_draw(keys[8], (HID,), 0.5, 3.0, (), jnp.float32)
    w_out = bell_draw(keys[9], (HID, D), HID ** -0.5, 0.1875)
    w_back = bell_draw(keys[10], (D, D), D ** -0.5, 0.25)
    grad_out = bell_draw(own_keys[11], (NODES, D), 1.0, 6.0, ((0, 16),))
    return dict(nodes=nodes, node_count=node_count, edge_src=edge_src, edge_dst=edge_dst, edge_count=edge_count, send_list=send_list, assign=assign, w_in=w_in, b_in=b_in, w_out=w_out, w_back=w_back, grad_out=grad_out)


def silu_grad(argument):
    squashed = jax.nn.sigmoid(argument)
    return squashed * (1.0 + argument * (1.0 - squashed))

def reference(nodes, node_count, edge_src, edge_dst, edge_count, send_list, assign, w_in, b_in, w_out, w_back, grad_out):
    node_ids = jnp.arange(NODES, dtype=jnp.int32)
    node_part = node_ids // NODE_DEV
    valid_rows = (node_ids % NODE_DEV < node_count[node_part]).astype(jnp.float32)[:, None]
    first_state = (nodes.astype(jnp.float32) * valid_rows).astype(jnp.bfloat16)
    edge_ids = jnp.arange(EDGES, dtype=jnp.int32)
    edge_part = edge_ids // EDGE_DEV
    edge_mask = (edge_ids % EDGE_DEV < edge_count[edge_part]).astype(jnp.float32)[:, None]
    shift_rows = jnp.array([-1, -1, -1, 0, 0, 1, 1, 1], dtype=jnp.int32)
    shift_cols = jnp.array([-1, 0, 1, -1, 1, -1, 0, 1], dtype=jnp.int32)
    is_local = edge_src < NODE_DEV
    halo_index = jnp.clip(edge_src - NODE_DEV, 0, NEIGHBOURS * SLOT - 1)
    direction = halo_index // SLOT
    slot_index = halo_index % SLOT
    neighbour = jnp.clip(edge_part + shift_rows[direction] * GRID_Y + shift_cols[direction], 0, PARTITIONS - 1)
    owner_row = send_list[neighbour, NEIGHBOURS - 1 - direction, slot_index]
    src_node = jnp.where(is_local, edge_part * NODE_DEV + edge_src, neighbour * NODE_DEV + owner_row).astype(jnp.int32)
    dst_node = (edge_part * NODE_DEV + edge_dst).astype(jnp.int32)
    weight_src = w_in[:D]
    weight_dst = w_in[D:]
    blocks = (src_node.reshape(PARTITIONS, EDGE_DEV), dst_node.reshape(PARTITIONS, EDGE_DEV), edge_mask.reshape(PARTITIONS, EDGE_DEV, 1))

    def edge_forward(block):
        src_ids, dst_ids, masks = block
        preact = jnp.dot(first_state[src_ids], weight_src, preferred_element_type=jnp.float32) + jnp.dot(first_state[dst_ids], weight_dst, preferred_element_type=jnp.float32) + b_in
        hidden = jax.nn.silu(preact).astype(jnp.bfloat16)
        return (jnp.dot(hidden, w_out, preferred_element_type=jnp.float32) * masks).astype(jnp.bfloat16)
    message = lax.map(edge_forward, blocks).reshape(EDGES, D)
    summed = jax.ops.segment_sum(message.astype(jnp.float32), dst_node, num_segments=NODES)
    mid_state = ((first_state.astype(jnp.float32) + summed) * valid_rows).astype(jnp.bfloat16)
    counts = jax.ops.segment_sum(valid_rows[:, 0], assign, num_segments=COARSE)
    inverse = 1.0 / jnp.maximum(counts, 1.0)
    pooled = jax.ops.segment_sum(mid_state.astype(jnp.float32) * valid_rows, assign, num_segments=COARSE)
    coarse = (pooled * inverse[:, None]).astype(jnp.bfloat16)
    spread = coarse[assign].astype(jnp.float32) * valid_rows
    lifted = jax.nn.silu(spread).astype(jnp.bfloat16)
    fields = ((mid_state.astype(jnp.float32) + jnp.dot(lifted, w_back, preferred_element_type=jnp.float32)) * valid_rows).astype(jnp.bfloat16)
    grad_top = (grad_out.astype(jnp.float32) * valid_rows).astype(jnp.bfloat16)
    grad_w_back = jnp.dot(lifted.T, grad_top, preferred_element_type=jnp.float32)
    grad_spread = jnp.dot(grad_top, w_back.T, preferred_element_type=jnp.float32) * silu_grad(spread)
    grad_coarse = jax.ops.segment_sum(grad_spread * valid_rows, assign, num_segments=COARSE) * inverse[:, None]
    grad_mid = ((grad_top.astype(jnp.float32) + grad_coarse[assign]) * valid_rows).astype(jnp.bfloat16)

    def edge_backward(carry, block):
        src_ids, dst_ids, masks = block
        src_rows = first_state[src_ids]
        dst_rows = first_state[dst_ids]
        preact = jnp.dot(src_rows, weight_src, preferred_element_type=jnp.float32) + jnp.dot(dst_rows, weight_dst, preferred_element_type=jnp.float32) + b_in
        hidden = jax.nn.silu(preact).astype(jnp.bfloat16)
        grad_msg = (grad_mid[dst_ids].astype(jnp.float32) * masks).astype(jnp.bfloat16)
        grad_pre = (jnp.dot(grad_msg, w_out.T, preferred_element_type=jnp.float32) * silu_grad(preact)).astype(jnp.bfloat16)
        part_in = jnp.concatenate([jnp.dot(src_rows.T, grad_pre, preferred_element_type=jnp.float32), jnp.dot(dst_rows.T, grad_pre, preferred_element_type=jnp.float32)], axis=0)
        part_bias = lax.optimization_barrier(jnp.sum(grad_pre.astype(jnp.float32), axis=0))
        part_out = jnp.dot(hidden.T, grad_msg, preferred_element_type=jnp.float32)
        grad_src = jnp.dot(grad_pre, weight_src.T, preferred_element_type=jnp.float32)
        grad_dst = jnp.dot(grad_pre, weight_dst.T, preferred_element_type=jnp.float32)
        return ((carry[0] + part_in, carry[1] + part_bias, carry[2] + part_out), (grad_src, grad_dst))
    start = (jnp.zeros((2 * D, HID), jnp.float32), jnp.zeros((HID,), jnp.float32), jnp.zeros((HID, D), jnp.float32))
    totals, grads = lax.scan(edge_backward, start, blocks)
    grad_src = grads[0].reshape(EDGES, D)
    grad_dst = grads[1].reshape(EDGES, D)
    grad_sum = grad_mid.astype(jnp.float32) + jax.ops.segment_sum(grad_src, src_node, num_segments=NODES) + jax.ops.segment_sum(grad_dst, dst_node, num_segments=NODES)
    grad_nodes = (grad_sum * valid_rows).astype(jnp.bfloat16)
    return (fields, grad_nodes, totals[0], totals[1], totals[2], grad_w_back)
```

```python
import functools

import jax
import jax.numpy as jnp
from jax import lax
from jax.experimental import pallas as pl
from jax.experimental.pallas import tpu as pltpu
from jax.sharding import PartitionSpec as P

GRID_Y = 8
CO_DEV = 4
MESH = pl.DeviceIdType.MESH
F32 = jnp.float32
BF16 = jnp.bfloat16
I32 = jnp.int32
directions = ((-1, -1), (-1, 0), (-1, 1), (0, -1), (0, 1), (1, -1), (1, 0), (1, 1))
pool_moves = ((2, 16, 8), (-2, 0, 8), (1, 8, 16), (-1, 0, 16))


def dot_nn(a, b):
    return jnp.dot(a, b, preferred_element_type=F32)


def dot_nt(a, b):
    return lax.dot_general(a, b, (((1,), (1,)), ((), ())), preferred_element_type=F32)


def dot_tn(a, b):
    return lax.dot_general(a, b, (((0,), (0,)), ((), ())), preferred_element_type=F32)


def sigmoid(v):
    return 0.5 * (1.0 + jnp.tanh(0.5 * v))


def as_columns(row):
    return jnp.transpose(jnp.broadcast_to(row, (128, row.shape[1])))


def hot_lanes(columns, start):
    lanes = lax.broadcasted_iota(I32, columns.shape, 1) + start
    return jnp.where(columns == lanes, 1.0, 0.0).astype(BF16)


def hot_rows(row, count):
    shape = (count, row.shape[1])
    return jnp.where(lax.broadcasted_iota(I32, shape, 0) == row, 1.0, 0.0).astype(BF16)


def scatters_inside(n, sizes):
    return n & (n - 1) == 0 and all(rows % (16 * n) == 0 for rows in sizes)


def kernel(n, inside, *refs):
    (
        nodes, node_count, edge_src, edge_dst, edge_count, send_rows, assign,
        w_in_hbm, b_in, w_out_hbm, w_back_hbm, grad_out,
        fields, grad_nodes, g_in, g_bias, g_out, g_back,
        w_in, w_out, w_back, load_sem,
        table, outgoing, halo_send, halo_recv,
        hot, hot_t, proj, slope, gathered, spread_sum,
        pool, pool_in, gpool, gpool_in, pool_send, pool_recv,
        back_out, back_in, back_send, back_recv,
        *scatter,
    ) = refs
    num_nodes, latent = nodes.shape
    num_edges = edge_src.shape[1]
    hid = b_in.shape[1]
    halo = send_rows.shape[1]
    slot = halo // len(directions)
    ext = num_nodes + halo
    me = lax.axis_index("dom")
    depth = n.bit_length() - 1

    loads = [
        pltpu.make_async_copy(source, target, load_sem.at[i])
        for i, (source, target) in enumerate(
            ((w_in_hbm, w_in), (w_out_hbm, w_out), (w_back_hbm, w_back))
        )
    ]
    for load in loads:
        load.start()

    def remote(source, target, sent, received, device):
        return pltpu.make_async_remote_copy(
            src_ref=source,
            dst_ref=target,
            send_sem=sent,
            recv_sem=received,
            device_id={"dom": device},
            device_id_type=MESH,
        )

    def beside(offset):
        return lax.rem(me + offset + 2 * n, n)

    table[num_nodes:, :] = jnp.zeros((halo, latent), BF16)
    back_in[...] = jnp.zeros((halo, latent), BF16)
    barrier = pltpu.get_barrier_semaphore()
    offsets = {(a * GRID_Y + b) % n for a, b in directions} | {1, 2, n - 1, n - 2}
    partners = [beside(offset) for offset in sorted(offsets)]
    if inside:
        for level in range(depth):
            step = 1 << level
            if step in offsets and n - step in offsets:
                continue
            partners.append(me + step - 2 * step * lax.rem(me // step, 2))
    for partner in partners:
        pl.semaphore_signal(barrier, inc=1, device_id={"dom": partner}, device_id_type=MESH)

    valid = lax.broadcasted_iota(I32, (num_nodes, 1), 0) < node_count[0]
    valid_f = jnp.where(valid, 1.0, 0.0)
    first = (nodes[...].astype(F32) * valid_f).astype(BF16)
    table[:num_nodes, :] = first
    send_cols = as_columns(send_rows[...])
    for start in range(0, num_nodes, 128):
        part = dot_nn(hot_lanes(send_cols, start), first[start : start + 128])
        sent = part if start == 0 else sent + part
    outgoing[...] = sent.astype(BF16)
    pl.semaphore_wait(barrier, len(partners))

    grid_row, grid_col = me // GRID_Y, lax.rem(me, GRID_Y)
    on_grid = [
        (grid_row + a >= 0)
        & (grid_row + a < n // GRID_Y)
        & (grid_col + b >= 0)
        & (grid_col + b < GRID_Y)
        for a, b in directions
    ]

    def halo_exchange(source, target, base, sent, received):
        copies = []
        for k, (a, b) in enumerate(directions):
            copy = remote(
                source.at[pl.ds(k * slot, slot)],
                target.at[pl.ds(base + (7 - k) * slot, slot)],
                sent.at[k],
                received.at[7 - k],
                beside(a * GRID_Y + b),
            )
            pl.when(on_grid[k])(copy.start)
            copies.append(copy)
        return copies

    def halo_wait(copies, recv):
        for k, copy in enumerate(copies):
            if recv:
                pl.when(on_grid[7 - k])(copy.wait_recv)
            else:
                pl.when(on_grid[k])(copy.wait_send)

    halo_copies = halo_exchange(outgoing, table, num_nodes, halo_send, halo_recv)

    edge_ok = lax.broadcasted_iota(I32, (1, num_edges), 1) < edge_count[0]
    src = jnp.where(edge_ok, edge_src[...], -1)
    dst = jnp.where(edge_ok, edge_dst[...], -1)
    hot_t[:ext, :] = hot_rows(src, ext)
    hot_t[ext:, :] = hot_rows(dst, num_nodes)
    src_cols, dst_cols = as_columns(src), as_columns(dst)
    for start in range(0, ext, 128):
        hot[:, start : start + 128] = hot_lanes(src_cols, start)
    for start in range(0, num_nodes, 128):
        hot[:, ext + start : ext + start + 128] = hot_lanes(dst_cols, start)

    total = CO_DEV * n
    rel = assign[...] - (me * CO_DEV - CO_DEV)
    rel = jnp.where(rel < 0, rel + total, rel)
    rel = jnp.where(rel >= total, rel - total, rel)
    node_ok = lax.broadcasted_iota(I32, (1, num_nodes), 1) < node_count[0]
    rel = jnp.where(node_ok, rel + (rel // CO_DEV) * (8 - CO_DEV), -100)
    window_hot = hot_rows(rel, 32)
    rel_cols = as_columns(rel)
    node_hot = hot_lanes(rel_cols, 0) + hot_lanes(rel_cols, -32)
    tail = jnp.zeros((64, latent), BF16)

    loads[0].wait()
    proj[:num_nodes, :] = dot_nn(first, w_in[:latent, :]).astype(BF16)
    proj[ext:, :] = dot_nn(first, w_in[latent:, :]).astype(BF16)
    halo_wait(halo_copies, True)
    proj[num_nodes:ext, :] = dot_nn(table[num_nodes:, :], w_in[:latent, :]).astype(BF16)

    wide = 256
    for start in range(0, hid, wide):
        cols = slice(start, start + wide)
        preact = dot_nn(hot[...], proj[:, cols]) + b_in[:, cols]
        gate = sigmoid(preact)
        hidden = preact * gate
        slope[:, cols] = gate + hidden * (1.0 - gate)
        gathered[:, cols] = dot_nn(hot_t[ext:, :], hidden.astype(BF16)).astype(BF16)
    loads[1].wait()
    summed = dot_nn(gathered[...], w_out[...])
    mid = ((first.astype(F32) + summed) * valid_f).astype(BF16)

    pool[:, :latent] = dot_nn(window_hot, mid)[:24]
    counts = jnp.sum(window_hot.astype(F32), axis=1, keepdims=True)
    pool[:, latent:] = jnp.broadcast_to(counts[:24], (24, 128))

    def pool_exchange(source, targets, level):
        copies = []
        for i, (offset, start, rows) in enumerate(pool_moves):
            copy = remote(
                source.at[pl.ds(start, rows)],
                targets.at[i, pl.ds(0, rows)],
                pool_send.at[level, i],
                pool_recv.at[level, i],
                beside(offset),
            )
            copy.start()
            copies.append(copy)
        return copies

    def pool_total(source, targets, copies):
        for copy in copies:
            copy.wait_recv()
        return (
            source[:8] + targets[2, :8] + targets[0, :8],
            source[8:16] + targets[2, 8:16] + targets[3, :8],
            source[16:24] + targets[3, 8:16] + targets[1, :8],
        )

    pool_copies = pool_exchange(pool, pool_in, 0)
    loads[2].wait()
    grad_top = (grad_out[...].astype(F32) * valid_f).astype(BF16)
    back_spread = dot_nt(grad_top, w_back[...])
    totals = jnp.concatenate(pool_total(pool, pool_in, pool_copies), axis=0)
    inverse = 1.0 / jnp.maximum(totals[:, latent : latent + 1], 1.0)
    coarse = totals[:, :latent] * inverse
    zeros8 = jnp.zeros((8, latent), F32)
    coarse = jnp.concatenate([coarse, zeros8], axis=0).astype(BF16)
    coarse = jnp.concatenate([coarse, jnp.zeros((32, latent), BF16), tail], axis=0)
    spread = dot_nn(node_hot, coarse)
    gate = sigmoid(spread)
    lifted_f = spread * gate
    grad_spread = back_spread * (gate + lifted_f * (1.0 - gate))
    gpool[...] = dot_nn(window_hot, grad_spread.astype(BF16))[:24]
    gpool_copies = pool_exchange(gpool, gpool_in, 1)
    lifted = lifted_f.astype(BF16)

    chunks = []
    if inside:
        bufs, ins, bias_buf, bias_in, sc_send, sc_recv, bias_send, bias_recv = (
            scatter[:4],
            scatter[4 : 4 + 4 * depth],
            *scatter[4 + 4 * depth :],
        )
        orders = [tuple(range(depth))] * 4
        bits = [lax.rem(me // (1 << level), 2) for level in range(depth)]

        def place(order, shard):
            return sum(((shard >> bit) & 1) << (depth - 1 - i) for i, bit in enumerate(order))

        pending = {}
        bases = [[0] * (depth + 1) for _ in range(4)]

        def send_half(c, level):
            order, half = orders[c], n >> (level + 1)
            bit = bits[order[level]]
            base = bases[c][level]
            bases[c][level + 1] = base + bit * half
            copy = remote(
                bufs[c].at[pl.ds(base + (1 - bit) * half, half)],
                ins[c * depth + level],
                sc_send.at[c, level],
                sc_recv.at[c, level],
                me + (1 - 2 * bit) * (1 << order[level]),
            )
            copy.start()
            pending[c, level] = copy

        def advance(c, level):
            pending[c, level].wait_recv()
            arrived = ins[c * depth + level]
            base = bases[c][level + 1]
            if level == depth - 1:
                return bufs[c][base].astype(F32) + arrived[0].astype(F32)
            half = n >> (level + 2)
            bit = bits[orders[c][level + 1]]

            def add(offset):
                target = pl.ds(base + offset, half)
                mine = bufs[c][target].astype(F32) + arrived[pl.ds(offset, half)].astype(F32)
                bufs[c][target] = mine.astype(BF16)

            add((1 - bit) * half)
            send_half(c, level + 1)
            add(bit * half)
            return None

        def store(c, value, cols):
            rows = value.shape[0] // n
            for shard in range(n):
                bufs[c][place(orders[c], shard), :, cols] = value[
                    shard * rows : (shard + 1) * rows
                ].astype(BF16)

    grad_back = dot_tn(lifted, grad_top)
    if inside:
        store(0, grad_back, slice(0, latent))
        send_half(0, 0)
    else:
        g_back[...] = grad_back
    top = mid.astype(F32) + dot_nn(lifted, w_back[...])
    fields[...] = (top * valid_f).astype(BF16)

    gsum = jnp.concatenate(pool_total(gpool, gpool_in, gpool_copies), axis=0) * inverse
    gsum = jnp.concatenate([gsum, zeros8], axis=0)
    upper = gsum.astype(BF16)
    lower = (gsum - upper.astype(F32)).astype(BF16)
    lifted_grad = dot_nn(node_hot, jnp.concatenate([upper, lower, tail], axis=0))
    grad_mid_f = (grad_top.astype(F32) + lifted_grad) * valid_f
    grad_mid = grad_mid_f.astype(BF16)
    if inside:
        advance(0, 0)
    grad_out_w = dot_tn(gathered[...], grad_mid)
    if inside:
        store(1, grad_out_w, slice(0, latent))
        send_half(1, 0)
    else:
        g_out[...] = grad_out_w

    sources = table[...]
    for start in range(0, hid, wide):
        cols = slice(start, start + wide)
        back = dot_nt(grad_mid, w_out[cols, :]).astype(BF16)
        grad_pre = (dot_nn(hot[:, ext:], back) * slope[:, cols]).astype(BF16)
        sums = dot_nn(hot_t[...], grad_pre).astype(BF16)
        spread_sum[:, cols] = sums
        partial = grad_pre.astype(F32).reshape(num_edges // 8, 8, wide).sum(axis=0)
        upper_grad = dot_tn(sources, sums[:ext])
        lower_grad = dot_tn(first, sums[ext:])
        if inside:
            bias_buf[0, :, cols] = partial
            c, left = 2 + start // latent, start % latent
            value = jnp.concatenate([upper_grad, lower_grad], axis=0)
            store(c, value, slice(left, left + wide))
            if left + wide == latent:
                send_half(c, 0)
            if start == 0:
                advance(1, 0)
                advance(0, 1)
            if start == 2 * wide:
                advance(1, 1)
                advance(2, 0)
                advance(0, 2)
        else:
            g_bias[:, cols] = partial
            g_in[:latent, cols] = upper_grad
            g_in[latent:, cols] = lower_grad

    def bias_level(level):
        step = 1 << level
        copy = remote(
            bias_buf.at[level],
            bias_in.at[level],
            bias_send.at[level],
            bias_recv.at[level],
            me + step - 2 * step * bits[level],
        )
        copy.start()
        return copy

    def bias_add(level, copy):
        copy.wait_recv()
        both = bias_buf[level] + bias_in[level]
        if level + 1 < depth:
            bias_buf[level + 1] = both
            return bias_level(level + 1)
        g_bias[...] = both
        return None

    halo_grad = dot_nt(spread_sum[num_nodes:ext, :], w_in[:latent, :])
    back_out[...] = halo_grad.astype(BF16)
    if inside:
        bias_copies = [bias_level(0)]
    back_copies = halo_exchange(back_out, back_in, 0, back_send, back_recv)
    if inside:
        advance(3, 0)
        advance(1, 2)
        advance(2, 1)
        bias_copies.append(bias_add(0, bias_copies[-1]))
    local = dot_nt(spread_sum[:num_nodes, :], w_in[:latent, :])
    local = local + dot_nt(spread_sum[ext:, :], w_in[latent:, :]) + grad_mid.astype(F32)
    if inside:
        g_back[...] = advance(0, depth - 1)
        bias_copies.append(bias_add(1, bias_copies[-1]))
    halo_wait(back_copies, True)
    owner_hot = hot_rows(send_rows[...], num_nodes)
    local = local + dot_nn(owner_hot, back_in[...])
    grad_nodes[...] = (local * valid_f).astype(BF16)
    if inside:
        advance(2, 2)
        advance(3, 1)
        g_out[...] = advance(1, depth - 1)
        bias_copies.append(bias_add(2, bias_copies[-1]))
        advance(3, 2)
        g_in[:, :latent] = advance(2, depth - 1)
        bias_add(3, bias_copies[-1])
        g_in[:, latent:] = advance(3, depth - 1)
        for copy in pending.values():
            copy.wait_send()
        for copy in bias_copies:
            copy.wait_send()
    halo_wait(halo_copies, False)
    halo_wait(back_copies, False)
    for copy in pool_copies + gpool_copies:
        copy.wait_send()


def body(
    nodes, node_count, edge_src, edge_dst, edge_count, send_list, assign,
    w_in, b_in, w_out, w_back, grad_out,
):
    num_nodes, latent = nodes.shape
    num_edges = edge_src.shape[0]
    hid = b_in.shape[0]
    n = lax.axis_size("dom")
    halo = send_list.shape[1] * send_list.shape[2]
    ext = num_nodes + halo
    inside = n == 16 and scatters_inside(n, (2 * latent, hid, latent))
    depth = n.bit_length() - 1
    share = n if inside else 1
    vmem = pl.BlockSpec(memory_space=pltpu.VMEM)
    smem = pl.BlockSpec(memory_space=pltpu.SMEM)
    anywhere = pl.BlockSpec(memory_space=pl.ANY)
    dma = pltpu.SemaphoreType.DMA
    scratch = [
        pltpu.VMEM(w_in.shape, BF16),
        pltpu.VMEM(w_out.shape, BF16),
        pltpu.VMEM(w_back.shape, BF16),
        dma((3,)),
        pltpu.VMEM((ext, latent), BF16),
        pltpu.VMEM((halo, latent), BF16),
        dma((8,)),
        dma((8,)),
        pltpu.VMEM((num_edges, ext + num_nodes), BF16),
        pltpu.VMEM((ext + num_nodes, num_edges), BF16),
        pltpu.VMEM((ext + num_nodes, hid), BF16),
        pltpu.VMEM((num_edges, hid), F32),
        pltpu.VMEM((num_nodes, hid), BF16),
        pltpu.VMEM((ext + num_nodes, hid), BF16),
        pltpu.VMEM((24, latent + 128), F32),
        pltpu.VMEM((4, 16, latent + 128), F32),
        pltpu.VMEM((24, latent), F32),
        pltpu.VMEM((4, 16, latent), F32),
        dma((2, 4)),
        dma((2, 4)),
        pltpu.VMEM((halo, latent), BF16),
        pltpu.VMEM((halo, latent), BF16),
        dma((8,)),
        dma((8,)),
    ]
    if inside:
        sizes = (latent, hid, 2 * latent, 2 * latent)
        scratch += [pltpu.VMEM((n, rows // n, latent), BF16) for rows in sizes]
        scratch += [
            pltpu.VMEM((n >> (level + 1), rows // n, latent), BF16)
            for rows in sizes
            for level in range(depth)
        ]
        scratch += [
            pltpu.VMEM((depth, 8, hid), F32),
            pltpu.VMEM((depth, 8, hid), F32),
            dma((4, depth)),
            dma((4, depth)),
            dma((depth,)),
            dma((depth,)),
        ]
    shapes = (
        jax.ShapeDtypeStruct((num_nodes, latent), BF16),
        jax.ShapeDtypeStruct((num_nodes, latent), BF16),
        jax.ShapeDtypeStruct((2 * latent // share, hid), F32),
        jax.ShapeDtypeStruct((8, hid), F32),
        jax.ShapeDtypeStruct((hid // share, latent), F32),
        jax.ShapeDtypeStruct((latent // share, latent), F32),
    )
    fields, grad_nodes, g_in, g_bias, g_out, g_back = pl.pallas_call(
        functools.partial(kernel, n, inside),
        out_shape=shapes,
        in_specs=[vmem, smem, vmem, vmem, smem, vmem, vmem, anywhere, vmem, anywhere, anywhere, vmem],
        out_specs=[vmem] * 6,
        scratch_shapes=scratch,
        compiler_params=pltpu.CompilerParams(
            collective_id=0, has_side_effects=True, vmem_limit_bytes=56 * 1024 * 1024
        ),
        name="mesh_step",
    )(
        nodes,
        node_count,
        edge_src.reshape(1, -1),
        edge_dst.reshape(1, -1),
        edge_count,
        send_list.reshape(1, -1),
        assign.reshape(1, -1),
        w_in,
        b_in.reshape(1, -1),
        w_out,
        w_back,
        grad_out,
    )
    bias = jnp.sum(g_bias, axis=0)
    if inside:
        width = hid // n
        bias = lax.dynamic_slice(bias, (lax.axis_index("dom") * width,), (width,))
        return fields, grad_nodes, g_in, bias, g_out, g_back
    summed = [
        lax.psum_scatter(value, "dom", scatter_dimension=0, tiled=True)
        for value in (g_in, bias, g_out, g_back)
    ]
    return (fields, grad_nodes, *summed)


def solution(mesh):
    rows = P(("parts", "dom"), None)
    line = P(("parts", "dom"))
    return jax.shard_map(
        body,
        mesh=mesh,
        in_specs=(
            rows, line, line, line, line, P(("parts", "dom"), None, None), line,
            P(), P(), P(), P(), rows,
        ),
        out_specs=(rows, rows, rows, line, rows, rows),
        check_vma=False,
    )
```

```python
import functools

import jax
import jax.numpy as jnp
from jax import lax
from jax.experimental import pallas as pl
from jax.experimental.pallas import tpu as pltpu
from jax.sharding import PartitionSpec as P

GRID_Y = 8
CO_DEV = 4
MESH = pl.DeviceIdType.MESH
F32 = jnp.float32
BF16 = jnp.bfloat16
I32 = jnp.int32
directions = ((-1, -1), (-1, 0), (-1, 1), (0, -1), (0, 1), (1, -1), (1, 0), (1, 1))
pool_moves = ((2, 16, 8), (-2, 0, 8), (1, 8, 16), (-1, 0, 16))


def dot_nn(a, b):
    return jnp.dot(a, b, preferred_element_type=F32)


def dot_nt(a, b):
    return lax.dot_general(a, b, (((1,), (1,)), ((), ())), preferred_element_type=F32)


def dot_tn(a, b):
    return lax.dot_general(a, b, (((0,), (0,)), ((), ())), preferred_element_type=F32)


def sigmoid(v):
    return 0.5 * (1.0 + jnp.tanh(0.5 * v))


def as_columns(row):
    return jnp.transpose(jnp.broadcast_to(row, (128, row.shape[1])))


def hot_lanes(columns, start):
    lanes = lax.broadcasted_iota(I32, columns.shape, 1) + start
    return jnp.where(columns == lanes, 1.0, 0.0).astype(BF16)


def hot_rows(row, count):
    shape = (count, row.shape[1])
    return jnp.where(lax.broadcasted_iota(I32, shape, 0) == row, 1.0, 0.0).astype(BF16)


def scatters_inside(n, sizes):
    return n & (n - 1) == 0 and all(rows % (16 * n) == 0 for rows in sizes)


def kernel(n, inside, *refs):
    (
        nodes_hbm, node_count, src_hbm, dst_hbm, edge_count, send_hbm, assign_hbm,
        w_in_hbm, b_in_hbm, w_out_hbm, w_back_hbm, grad_out_hbm,
        fields, grad_nodes, g_in, g_bias, g_out, g_back,
        w_in, w_out, w_back, nodes, edge_src, edge_dst, send_list, assign, b_in, grad_out, load_sem,
        table, outgoing, halo_send, halo_recv,
        table_t, gathered_t, hot, hot_t, proj, slope, gathered, spread_sum,
        pool, pool_in, gpool, gpool_in, pool_send, pool_recv,
        back_out, back_in, back_send, back_recv,
        *scatter,
    ) = refs
    num_nodes, latent = nodes.shape
    num_edges = edge_src.shape[1]
    hid = b_in.shape[1]
    slot = send_list.shape[2]
    halo = len(directions) * slot
    ext = num_nodes + halo
    me = lax.axis_index("dom")
    depth = n.bit_length() - 1

    def remote(source, target, sent, received, device):
        return pltpu.make_async_remote_copy(
            src_ref=source,
            dst_ref=target,
            send_sem=sent,
            recv_sem=received,
            device_id={"dom": device},
            device_id_type=MESH,
        )

    def beside(offset):
        return lax.rem(me + offset + 2 * n, n)

    loads = [
        pltpu.make_async_copy(source, target, load_sem.at[i])
        for i, (source, target) in enumerate(
            (
                (w_in_hbm, w_in),
                (w_out_hbm, w_out),
                (w_back_hbm, w_back),
                (nodes_hbm, nodes),
                (send_hbm, send_list),
                (src_hbm, edge_src),
                (dst_hbm, edge_dst),
                (assign_hbm, assign),
                (b_in_hbm, b_in),
                (grad_out_hbm, grad_out),
            )
        )
    ]
    for i in (3, 4, 5, 6, 7, 8, 0, 1, 2, 9):
        loads[i].start()
    table[num_nodes:, :] = jnp.zeros((halo, latent), BF16)
    back_in[...] = jnp.zeros((halo, latent), BF16)
    barrier = pltpu.get_barrier_semaphore()
    offsets = {(a * GRID_Y + b) % n for a, b in directions} | {1, 2, n - 1, n - 2}
    partners = [beside(offset) for offset in sorted(offsets)]
    if inside:
        for level in range(depth):
            step = 1 << level
            if step in offsets and n - step in offsets:
                continue
            partners.append(me + step - 2 * step * lax.rem(me // step, 2))
    for partner in partners:
        pl.semaphore_signal(barrier, inc=1, device_id={"dom": partner}, device_id_type=MESH)

    valid = lax.broadcasted_iota(I32, (num_nodes, 1), 0) < node_count[0]
    valid_f = jnp.where(valid, 1.0, 0.0)
    loads[3].wait()
    loads[4].wait()
    first = (nodes[...].astype(F32) * valid_f).astype(BF16)
    table[:num_nodes, :] = first
    send_rows = jnp.concatenate([send_list[0, k : k + 1, :] for k in range(8)], axis=1)
    send_cols = as_columns(send_rows)
    for start in range(0, num_nodes, 128):
        part = dot_nn(hot_lanes(send_cols, start), first[start : start + 128])
        sent = part if start == 0 else sent + part
    outgoing[...] = sent.astype(BF16)
    pl.semaphore_wait(barrier, len(partners))

    grid_row, grid_col = me // GRID_Y, lax.rem(me, GRID_Y)
    on_grid = [
        (grid_row + a >= 0)
        & (grid_row + a < n // GRID_Y)
        & (grid_col + b >= 0)
        & (grid_col + b < GRID_Y)
        for a, b in directions
    ]

    def halo_exchange(source, target, base, sent, received):
        copies = []
        for k, (a, b) in enumerate(directions):
            copy = remote(
                source.at[pl.ds(k * slot, slot)],
                target.at[pl.ds(base + (7 - k) * slot, slot)],
                sent.at[k],
                received.at[7 - k],
                beside(a * GRID_Y + b),
            )
            pl.when(on_grid[k])(copy.start)
            copies.append(copy)
        return copies

    def halo_wait(copies, recv):
        for k, copy in enumerate(copies):
            if recv:
                pl.when(on_grid[7 - k])(copy.wait_recv)
            else:
                pl.when(on_grid[k])(copy.wait_send)

    halo_copies = halo_exchange(outgoing, table, num_nodes, halo_send, halo_recv)

    for i in (5, 6, 7, 8):
        loads[i].wait()
    edge_ok = lax.broadcasted_iota(I32, (1, num_edges), 1) < edge_count[0]
    src = jnp.where(edge_ok, edge_src[...], -1)
    dst = jnp.where(edge_ok, edge_dst[...], -1)
    hot_t[:ext, :] = hot_rows(src, ext)
    hot_t[ext:, :] = hot_rows(dst, num_nodes)
    src_cols, dst_cols = as_columns(src), as_columns(dst)
    for start in range(0, ext, 128):
        hot[:, start : start + 128] = hot_lanes(src_cols, start)
    for start in range(0, num_nodes, 128):
        hot[:, ext + start : ext + start + 128] = hot_lanes(dst_cols, start)

    total = CO_DEV * n
    rel = assign[...] - (me * CO_DEV - CO_DEV)
    rel = jnp.where(rel < 0, rel + total, rel)
    rel = jnp.where(rel >= total, rel - total, rel)
    node_ok = lax.broadcasted_iota(I32, (1, num_nodes), 1) < node_count[0]
    rel = jnp.where(node_ok, rel + (rel // CO_DEV) * (8 - CO_DEV), -100)
    window_hot = hot_rows(rel, 32)
    rel_cols = as_columns(rel)
    node_hot = hot_lanes(rel_cols, 0) + hot_lanes(rel_cols, -32)
    tail = jnp.zeros((64, latent), BF16)

    loads[0].wait()
    proj[:num_nodes, :] = dot_nn(first, w_in[:latent, :]).astype(BF16)
    proj[ext:, :] = dot_nn(first, w_in[latent:, :]).astype(BF16)
    halo_wait(halo_copies, True)
    proj[num_nodes:ext, :] = dot_nn(table[num_nodes:, :], w_in[:latent, :]).astype(BF16)

    wide = 256
    for start in range(0, hid, wide):
        cols = slice(start, start + wide)
        preact = dot_nn(hot[...], proj[:, cols]) + b_in[:, cols]
        slope[:, cols] = preact
        hidden = preact * sigmoid(preact)
        gathered[:, cols] = dot_nn(hot_t[ext:, :], hidden.astype(BF16)).astype(BF16)
    loads[1].wait()
    summed = dot_nn(gathered[...], w_out[...])
    mid = ((first.astype(F32) + summed) * valid_f).astype(BF16)

    pool[:, :latent] = dot_nn(window_hot, mid)[:24]
    counts = jnp.sum(window_hot.astype(F32), axis=1, keepdims=True)
    pool[:, latent:] = jnp.broadcast_to(counts[:24], (24, 128))

    def pool_exchange(source, targets, level):
        copies = []
        for i, (offset, start, rows) in enumerate(pool_moves):
            copy = remote(
                source.at[pl.ds(start, rows)],
                targets.at[i, pl.ds(0, rows)],
                pool_send.at[level, i],
                pool_recv.at[level, i],
                beside(offset),
            )
            copy.start()
            copies.append(copy)
        return copies

    def pool_total(source, targets, copies):
        for copy in copies:
            copy.wait_recv()
        return (
            source[:8] + targets[2, :8] + targets[0, :8],
            source[8:16] + targets[2, 8:16] + targets[3, :8],
            source[16:24] + targets[3, 8:16] + targets[1, :8],
        )

    def finish_slope(start):
        for left in range(start, start + hid // 2, wide):
            cols = slice(left, left + wide)
            preact = slope[:, cols]
            gate = sigmoid(preact)
            slope[:, cols] = gate + preact * gate * (1.0 - gate)

    pool_copies = pool_exchange(pool, pool_in, 0)
    loads[2].wait()
    loads[9].wait()
    grad_top = (grad_out[...].astype(F32) * valid_f).astype(BF16)
    back_spread = dot_nt(grad_top, w_back[...])
    table_t[...] = jnp.transpose(table[...])
    gathered_t[...] = jnp.transpose(gathered[...])
    finish_slope(0)
    totals = jnp.concatenate(pool_total(pool, pool_in, pool_copies), axis=0)
    inverse = 1.0 / jnp.maximum(totals[:, latent : latent + 1], 1.0)
    coarse = totals[:, :latent] * inverse
    zeros8 = jnp.zeros((8, latent), F32)
    coarse = jnp.concatenate([coarse, zeros8], axis=0).astype(BF16)
    coarse = jnp.concatenate([coarse, jnp.zeros((32, latent), BF16), tail], axis=0)
    spread = dot_nn(node_hot, coarse)
    gate = sigmoid(spread)
    lifted_f = spread * gate
    grad_spread = back_spread * (gate + lifted_f * (1.0 - gate))
    gpool[...] = dot_nn(window_hot, grad_spread.astype(BF16))[:24]
    gpool_copies = pool_exchange(gpool, gpool_in, 1)
    lifted = lifted_f.astype(BF16)

    chunks = []
    if inside:
        bufs, ins, bias_buf, bias_in, sc_send, sc_recv, bias_send, bias_recv = (
            scatter[:6],
            scatter[6 : 6 + 6 * depth],
            *scatter[6 + 6 * depth :],
        )
        orders = [(0, 1, 2, 3), (0, 2, 1, 3), (0, 1, 2, 3), (0, 1, 2, 3), (0, 2, 1, 3), (0, 1, 2, 3)]
        bits = [lax.rem(me // (1 << level), 2) for level in range(depth)]

        def place(order, shard):
            return sum(((shard >> bit) & 1) << (depth - 1 - i) for i, bit in enumerate(order))

        pending = {}
        bases = [[0] * (depth + 1) for _ in range(6)]

        def send_half(c, level):
            order, half = orders[c], n >> (level + 1)
            bit = bits[order[level]]
            base = bases[c][level]
            bases[c][level + 1] = base + bit * half
            copy = remote(
                bufs[c].at[pl.ds(base + (1 - bit) * half, half)],
                ins[c * depth + level],
                sc_send.at[c, level],
                sc_recv.at[c, level],
                me + (1 - 2 * bit) * (1 << order[level]),
            )
            copy.start()
            pending[c, level] = copy

        def advance(c, level):
            pending[c, level].wait_recv()
            arrived = ins[c * depth + level]
            base = bases[c][level + 1]
            if level == depth - 1:
                return bufs[c][base].astype(F32) + arrived[0].astype(F32)
            half = n >> (level + 2)
            bit = bits[orders[c][level + 1]]

            def add(offset):
                target = pl.ds(base + offset, half)
                mine = bufs[c][target].astype(F32) + arrived[pl.ds(offset, half)].astype(F32)
                bufs[c][target] = mine.astype(BF16)

            add((1 - bit) * half)
            send_half(c, level + 1)
            add(bit * half)
            return None

        def store(c, value):
            rows = value.shape[0] // n
            for shard in range(n):
                bufs[c][place(orders[c], shard)] = value[
                    shard * rows : (shard + 1) * rows
                ].astype(BF16)

    grad_back = dot_tn(lifted, grad_top)
    if inside:
        store(0, grad_back)
        send_half(0, 0)
    else:
        g_back[...] = grad_back
    top = mid.astype(F32) + dot_nn(lifted, w_back[...])
    fields[...] = (top * valid_f).astype(BF16)

    finish_slope(hid // 2)
    gsum = jnp.concatenate(pool_total(gpool, gpool_in, gpool_copies), axis=0) * inverse
    gsum = jnp.concatenate([gsum, zeros8], axis=0)
    upper = gsum.astype(BF16)
    lower = (gsum - upper.astype(F32)).astype(BF16)
    lifted_grad = dot_nn(node_hot, jnp.concatenate([upper, lower, tail], axis=0))
    grad_mid_f = (grad_top.astype(F32) + lifted_grad) * valid_f
    grad_mid = grad_mid_f.astype(BF16)
    if inside:
        advance(0, 0)
    grad_out_w = dot_nn(gathered_t[...], grad_mid)
    if inside:
        store(1, grad_out_w)
        send_half(1, 0)
    else:
        g_out[...] = grad_out_w

    for start in range(0, hid, wide):
        cols = slice(start, start + wide)
        back = dot_nt(grad_mid, w_out[cols, :]).astype(BF16)
        grad_pre = (dot_nn(hot[:, ext:], back) * slope[:, cols]).astype(BF16)
        sums = dot_nn(hot_t[...], grad_pre).astype(BF16)
        spread_sum[:, cols] = sums
        partial = grad_pre.astype(F32).reshape(num_edges // 8, 8, wide).sum(axis=0)
        upper_grad = dot_nn(table_t[...], sums[:ext])
        lower_grad = dot_nn(table_t[:, :num_nodes], sums[ext:])
        if inside:
            bias_buf[0, :, cols] = partial
            c = 2 + start // wide
            store(c, jnp.concatenate([upper_grad, lower_grad], axis=0))
            send_half(c, 0)
            for step in (((1, 0),), ((0, 1), (2, 0)), ((1, 1), (3, 0)), ((0, 2), (2, 1), (4, 0)))[c - 2]:
                advance(*step)
        else:
            g_bias[:, cols] = partial
            g_in[:latent, cols] = upper_grad
            g_in[latent:, cols] = lower_grad

    def bias_level(level):
        step = 1 << level
        copy = remote(
            bias_buf.at[level],
            bias_in.at[level],
            bias_send.at[level],
            bias_recv.at[level],
            me + step - 2 * step * bits[level],
        )
        copy.start()
        return copy

    def bias_add(level, copy):
        copy.wait_recv()
        both = bias_buf[level] + bias_in[level]
        if level + 1 < depth:
            bias_buf[level + 1] = both
            return bias_level(level + 1)
        g_bias[...] = both
        return None

    halo_grad = dot_nt(spread_sum[num_nodes:ext, :], w_in[:latent, :])
    back_out[...] = halo_grad.astype(BF16)
    if inside:
        bias_copies = [bias_level(0)]
    back_copies = halo_exchange(back_out, back_in, 0, back_send, back_recv)
    if inside:
        advance(5, 0)
        advance(1, 2)
        advance(3, 1)
        bias_copies.append(bias_add(0, bias_copies[-1]))
    local = dot_nt(spread_sum[:num_nodes, :], w_in[:latent, :])
    local = local + dot_nt(spread_sum[ext:, :], w_in[latent:, :]) + grad_mid.astype(F32)
    if inside:
        g_back[...] = advance(0, depth - 1)
        advance(4, 1)
        advance(2, 2)
    halo_wait(back_copies, True)
    owner_hot = hot_rows(send_rows, num_nodes)
    local = local + dot_nn(owner_hot, back_in[...])
    grad_nodes[...] = (local * valid_f).astype(BF16)
    if inside:
        g_out[...] = advance(1, depth - 1)
        advance(5, 1)
        bias_copies.append(bias_add(1, bias_copies[-1]))
        advance(3, 2)
        advance(4, 2)
        g_in[:, :wide] = advance(2, depth - 1)
        bias_copies.append(bias_add(2, bias_copies[-1]))
        advance(5, 2)
        g_in[:, wide : 2 * wide] = advance(3, depth - 1)
        g_in[:, 2 * wide : 3 * wide] = advance(4, depth - 1)
        bias_add(3, bias_copies[-1])
        g_in[:, 3 * wide :] = advance(5, depth - 1)
        for copy in pending.values():
            copy.wait_send()
        for copy in bias_copies:
            copy.wait_send()
    halo_wait(halo_copies, False)
    halo_wait(back_copies, False)
    for copy in pool_copies + gpool_copies:
        copy.wait_send()


def finish(n, g_bias, *refs):
    wholes, results, bias, sem = refs[:5], refs[5:10], refs[10], refs[11]
    copies = [
        pltpu.make_async_copy(source, target, sem.at[i])
        for i, (source, target) in enumerate(zip(wholes, results))
    ]
    for copy in copies:
        copy.start()
    line = jnp.sum(g_bias[...], axis=0, keepdims=True)
    width = line.shape[1] // n
    me = lax.axis_index("dom")
    shards = [line[:, i * width : (i + 1) * width] for i in range(n)]
    mine = jnp.where(me == 0, shards[0], 0.0)
    for i in range(1, n):
        mine = jnp.where(me == i, shards[i], mine)
    bias[...] = mine.reshape(width)
    for copy in copies:
        copy.wait()


def body(
    nodes, node_count, edge_src, edge_dst, edge_count, send_list, assign,
    w_in, b_in, w_out, w_back, grad_out,
):
    num_nodes, latent = nodes.shape
    num_edges = edge_src.shape[0]
    hid = b_in.shape[0]
    n = lax.axis_size("dom")
    halo = send_list.shape[1] * send_list.shape[2]
    ext = num_nodes + halo
    inside = n == 16 and scatters_inside(n, (2 * latent, hid, latent))
    depth = n.bit_length() - 1
    share = n if inside else 1
    vmem = pl.BlockSpec(memory_space=pltpu.VMEM)
    smem = pl.BlockSpec(memory_space=pltpu.SMEM)
    anywhere = pl.BlockSpec(memory_space=pl.ANY)
    dma = pltpu.SemaphoreType.DMA
    scratch = [
        pltpu.VMEM(w_in.shape, BF16),
        pltpu.VMEM(w_out.shape, BF16),
        pltpu.VMEM(w_back.shape, BF16),
        pltpu.VMEM(nodes.shape, BF16),
        pltpu.VMEM((1, num_edges), I32),
        pltpu.VMEM((1, num_edges), I32),
        pltpu.VMEM(send_list.shape, I32),
        pltpu.VMEM((1, num_nodes), I32),
        pltpu.VMEM((1, hid), F32),
        pltpu.VMEM(grad_out.shape, BF16),
        dma((10,)),
        pltpu.VMEM((ext, latent), BF16),
        pltpu.VMEM((halo, latent), BF16),
        dma((8,)),
        dma((8,)),
        pltpu.VMEM((latent, ext), BF16),
        pltpu.VMEM((hid, num_nodes), BF16),
        pltpu.VMEM((num_edges, ext + num_nodes), BF16),
        pltpu.VMEM((ext + num_nodes, num_edges), BF16),
        pltpu.VMEM((ext + num_nodes, hid), BF16),
        pltpu.VMEM((num_edges, hid), F32),
        pltpu.VMEM((num_nodes, hid), BF16),
        pltpu.VMEM((ext + num_nodes, hid), BF16),
        pltpu.VMEM((24, latent + 128), F32),
        pltpu.VMEM((4, 16, latent + 128), F32),
        pltpu.VMEM((24, latent), F32),
        pltpu.VMEM((4, 16, latent), F32),
        dma((2, 4)),
        dma((2, 4)),
        pltpu.VMEM((halo, latent), BF16),
        pltpu.VMEM((halo, latent), BF16),
        dma((8,)),
        dma((8,)),
    ]
    if inside:
        sizes = ((latent, latent), (hid, latent)) + ((2 * latent, 256),) * 4
        scratch += [pltpu.VMEM((n, rows // n, cols), BF16) for rows, cols in sizes]
        scratch += [
            pltpu.VMEM((n >> (level + 1), rows // n, cols), BF16)
            for rows, cols in sizes
            for level in range(depth)
        ]
        scratch += [
            pltpu.VMEM((depth, 8, hid), F32),
            pltpu.VMEM((depth, 8, hid), F32),
            dma((6, depth)),
            dma((6, depth)),
            dma((depth,)),
            dma((depth,)),
        ]
    shapes = (
        jax.ShapeDtypeStruct((num_nodes, latent), BF16),
        jax.ShapeDtypeStruct((num_nodes, latent), BF16),
        jax.ShapeDtypeStruct((2 * latent // share, hid), F32),
        jax.ShapeDtypeStruct((8, hid), F32),
        jax.ShapeDtypeStruct((hid // share, latent), F32),
        jax.ShapeDtypeStruct((latent // share, latent), F32),
    )
    fields, grad_nodes, g_in, g_bias, g_out, g_back = pl.pallas_call(
        functools.partial(kernel, n, inside),
        out_shape=shapes,
        in_specs=[anywhere, smem, anywhere, anywhere, smem] + [anywhere] * 7,
        out_specs=[vmem] * 6,
        scratch_shapes=scratch,
        compiler_params=pltpu.CompilerParams(
            collective_id=0, has_side_effects=True, vmem_limit_bytes=56 * 1024 * 1024
        ),
        name="mesh_step",
    )(
        nodes,
        node_count,
        edge_src.reshape(1, -1),
        edge_dst.reshape(1, -1),
        edge_count,
        send_list,
        assign.reshape(1, -1),
        w_in,
        b_in.reshape(1, -1),
        w_out,
        w_back,
        grad_out,
    )
    if inside:
        wholes = (fields, grad_nodes, g_in, g_out, g_back)
        fields, grad_nodes, g_in, g_out, g_back, bias = pl.pallas_call(
            functools.partial(finish, n),
            out_shape=[jax.ShapeDtypeStruct(whole.shape, whole.dtype) for whole in wholes]
            + [jax.ShapeDtypeStruct((hid // n,), F32)],
            in_specs=[vmem] * 6,
            out_specs=[anywhere] * 5 + [vmem],
            scratch_shapes=[dma((5,))],
            name="place_results",
        )(g_bias, *wholes)
        return fields, grad_nodes, g_in, bias, g_out, g_back
    bias = jnp.sum(g_bias, axis=0)
    summed = [
        lax.psum_scatter(value, "dom", scatter_dimension=0, tiled=True)
        for value in (g_in, bias, g_out, g_back)
    ]
    return (fields, grad_nodes, *summed)


def solution(mesh):
    rows = P(("parts", "dom"), None)
    line = P(("parts", "dom"))
    return jax.shard_map(
        body,
        mesh=mesh,
        in_specs=(
            rows, line, line, line, line, P(("parts", "dom"), None, None), line,
            P(), P(), P(), P(), rows,
        ),
        out_specs=(rows, rows, rows, line, rows, rows),
        check_vma=False,
    )
```

```python
import functools

import jax
import jax.numpy as jnp
from jax import lax
from jax.experimental import pallas as pl
from jax.experimental.pallas import tpu as pltpu
from jax.sharding import PartitionSpec as P

GRID_Y = 8
CO_DEV = 4
MESH = pl.DeviceIdType.MESH
F32 = jnp.float32
BF16 = jnp.bfloat16
I32 = jnp.int32
directions = ((-1, -1), (-1, 0), (-1, 1), (0, -1), (0, 1), (1, -1), (1, 0), (1, 1))
pool_moves = ((2, 16, 8), (-2, 0, 8), (1, 8, 16), (-1, 0, 16))


def dot_nn(a, b):
    return jnp.dot(a, b, preferred_element_type=F32)


def dot_nt(a, b):
    return lax.dot_general(a, b, (((1,), (1,)), ((), ())), preferred_element_type=F32)


def dot_tn(a, b):
    return lax.dot_general(a, b, (((0,), (0,)), ((), ())), preferred_element_type=F32)


def sigmoid(v):
    return 0.5 * (1.0 + jnp.tanh(0.5 * v))


def as_columns(row):
    return jnp.transpose(jnp.broadcast_to(row, (128, row.shape[1])))


def hot_lanes(columns, start):
    lanes = lax.broadcasted_iota(I32, columns.shape, 1) + start
    return jnp.where(columns == lanes, 1.0, 0.0).astype(BF16)


def hot_rows(row, count):
    shape = (count, row.shape[1])
    return jnp.where(lax.broadcasted_iota(I32, shape, 0) == row, 1.0, 0.0).astype(BF16)


def scatters_inside(n, sizes):
    return n & (n - 1) == 0 and all(rows % (16 * n) == 0 for rows in sizes)


def kernel(n, inside, *refs):
    (
        nodes_hbm, node_count, src_hbm, dst_hbm, edge_count, send_hbm, assign_hbm,
        w_in_hbm, b_in_hbm, w_out_hbm, w_back_hbm, grad_out_hbm,
        fields, grad_nodes, g_in, g_bias, g_out, g_back,
        w_in, w_out, w_back, nodes, edge_src, edge_dst, send_list, assign, b_in, grad_out, load_sem,
        table, outgoing, halo_send, halo_recv,
        table_t, gathered_t, hot, hot_t, proj, slope, gathered, spread_sum,
        pool, pool_in, gpool, gpool_in, pool_send, pool_recv,
        back_out, back_in, back_send, back_recv,
        *scatter,
    ) = refs
    num_nodes, latent = nodes.shape
    num_edges = edge_src.shape[1]
    hid = b_in.shape[1]
    slot = send_list.shape[2]
    halo = len(directions) * slot
    ext = num_nodes + halo
    me = lax.axis_index("dom")
    depth = n.bit_length() - 1

    def remote(source, target, sent, received, device):
        return pltpu.make_async_remote_copy(
            src_ref=source,
            dst_ref=target,
            send_sem=sent,
            recv_sem=received,
            device_id={"dom": device},
            device_id_type=MESH,
        )

    def beside(offset):
        return lax.rem(me + offset + 2 * n, n)

    loads = [
        pltpu.make_async_copy(source, target, load_sem.at[i])
        for i, (source, target) in enumerate(
            (
                (w_in_hbm, w_in),
                (w_out_hbm, w_out),
                (w_back_hbm, w_back),
                (nodes_hbm, nodes),
                (send_hbm, send_list),
                (src_hbm, edge_src),
                (dst_hbm, edge_dst),
                (assign_hbm, assign),
                (b_in_hbm, b_in),
                (grad_out_hbm, grad_out),
            )
        )
    ]
    for i in (3, 4, 5, 6, 7, 8, 0, 1, 2, 9):
        loads[i].start()
    table[num_nodes:, :] = jnp.zeros((halo, latent), BF16)
    back_in[...] = jnp.zeros((halo, latent), BF16)
    barrier = pltpu.get_barrier_semaphore()
    offsets = {(a * GRID_Y + b) % n for a, b in directions} | {1, 2, n - 1, n - 2}
    if inside:
        offsets = set(range(1, n))
    partners = [beside(offset) for offset in sorted(offsets)]
    for partner in partners:
        pl.semaphore_signal(barrier, inc=1, device_id={"dom": partner}, device_id_type=MESH)

    valid = lax.broadcasted_iota(I32, (num_nodes, 1), 0) < node_count[0]
    valid_f = jnp.where(valid, 1.0, 0.0)
    loads[3].wait()
    loads[4].wait()
    first = (nodes[...].astype(F32) * valid_f).astype(BF16)
    table[:num_nodes, :] = first
    send_rows = jnp.concatenate([send_list[0, k : k + 1, :] for k in range(8)], axis=1)
    send_cols = as_columns(send_rows)
    for start in range(0, num_nodes, 128):
        part = dot_nn(hot_lanes(send_cols, start), first[start : start + 128])
        sent = part if start == 0 else sent + part
    outgoing[...] = sent.astype(BF16)
    pl.semaphore_wait(barrier, len(partners))

    grid_row, grid_col = me // GRID_Y, lax.rem(me, GRID_Y)
    on_grid = [
        (grid_row + a >= 0)
        & (grid_row + a < n // GRID_Y)
        & (grid_col + b >= 0)
        & (grid_col + b < GRID_Y)
        for a, b in directions
    ]

    def halo_exchange(source, target, base, sent, received):
        copies = []
        for k, (a, b) in enumerate(directions):
            copy = remote(
                source.at[pl.ds(k * slot, slot)],
                target.at[pl.ds(base + (7 - k) * slot, slot)],
                sent.at[k],
                received.at[7 - k],
                beside(a * GRID_Y + b),
            )
            pl.when(on_grid[k])(copy.start)
            copies.append(copy)
        return copies

    def halo_wait(copies, recv):
        for k, copy in enumerate(copies):
            if recv:
                pl.when(on_grid[7 - k])(copy.wait_recv)
            else:
                pl.when(on_grid[k])(copy.wait_send)

    halo_copies = halo_exchange(outgoing, table, num_nodes, halo_send, halo_recv)

    for i in (5, 6, 7, 8):
        loads[i].wait()
    edge_ok = lax.broadcasted_iota(I32, (1, num_edges), 1) < edge_count[0]
    src = jnp.where(edge_ok, edge_src[...], -1)
    dst = jnp.where(edge_ok, edge_dst[...], -1)
    hot_t[:ext, :] = hot_rows(src, ext)
    hot_t[ext:, :] = hot_rows(dst, num_nodes)
    src_cols, dst_cols = as_columns(src), as_columns(dst)
    for start in range(0, ext, 128):
        hot[:, start : start + 128] = hot_lanes(src_cols, start)
    for start in range(0, num_nodes, 128):
        hot[:, ext + start : ext + start + 128] = hot_lanes(dst_cols, start)

    total = CO_DEV * n
    rel = assign[...] - (me * CO_DEV - CO_DEV)
    rel = jnp.where(rel < 0, rel + total, rel)
    rel = jnp.where(rel >= total, rel - total, rel)
    node_ok = lax.broadcasted_iota(I32, (1, num_nodes), 1) < node_count[0]
    rel = jnp.where(node_ok, rel + (rel // CO_DEV) * (8 - CO_DEV), -100)
    window_hot = hot_rows(rel, 32)
    rel_cols = as_columns(rel)
    node_hot = hot_lanes(rel_cols, 0) + hot_lanes(rel_cols, -32)
    tail = jnp.zeros((64, latent), BF16)

    loads[0].wait()
    proj[:num_nodes, :] = dot_nn(first, w_in[:latent, :]).astype(BF16)
    proj[ext:, :] = dot_nn(first, w_in[latent:, :]).astype(BF16)
    halo_wait(halo_copies, True)
    proj[num_nodes:ext, :] = dot_nn(table[num_nodes:, :], w_in[:latent, :]).astype(BF16)

    wide = 256
    for start in range(0, hid, wide):
        cols = slice(start, start + wide)
        preact = dot_nn(hot[...], proj[:, cols]) + b_in[:, cols]
        slope[:, cols] = preact
        hidden = preact * sigmoid(preact)
        gathered[:, cols] = dot_nn(hot_t[ext:, :], hidden.astype(BF16)).astype(BF16)
    loads[1].wait()
    summed = dot_nn(gathered[...], w_out[...])
    mid = ((first.astype(F32) + summed) * valid_f).astype(BF16)

    pool[:, :latent] = dot_nn(window_hot, mid)[:24]
    counts = jnp.sum(window_hot.astype(F32), axis=1, keepdims=True)
    pool[:, latent:] = jnp.broadcast_to(counts[:24], (24, 128))

    def pool_exchange(source, targets, level):
        copies = []
        for i, (offset, start, rows) in enumerate(pool_moves):
            copy = remote(
                source.at[pl.ds(start, rows)],
                targets.at[i, pl.ds(0, rows)],
                pool_send.at[level, i],
                pool_recv.at[level, i],
                beside(offset),
            )
            copy.start()
            copies.append(copy)
        return copies

    def pool_total(source, targets, copies):
        for copy in copies:
            copy.wait_recv()
        return (
            source[:8] + targets[2, :8] + targets[0, :8],
            source[8:16] + targets[2, 8:16] + targets[3, :8],
            source[16:24] + targets[3, 8:16] + targets[1, :8],
        )

    def finish_slope(start):
        for left in range(start, start + hid // 2, wide):
            cols = slice(left, left + wide)
            preact = slope[:, cols]
            gate = sigmoid(preact)
            slope[:, cols] = gate + preact * gate * (1.0 - gate)

    pool_copies = pool_exchange(pool, pool_in, 0)
    loads[2].wait()
    loads[9].wait()
    grad_top = (grad_out[...].astype(F32) * valid_f).astype(BF16)
    back_spread = dot_nt(grad_top, w_back[...])
    table_t[...] = jnp.transpose(table[...])
    gathered_t[...] = jnp.transpose(gathered[...])
    finish_slope(0)
    totals = jnp.concatenate(pool_total(pool, pool_in, pool_copies), axis=0)
    inverse = 1.0 / jnp.maximum(totals[:, latent : latent + 1], 1.0)
    coarse = totals[:, :latent] * inverse
    zeros8 = jnp.zeros((8, latent), F32)
    coarse = jnp.concatenate([coarse, zeros8], axis=0).astype(BF16)
    coarse = jnp.concatenate([coarse, jnp.zeros((32, latent), BF16), tail], axis=0)
    spread = dot_nn(node_hot, coarse)
    gate = sigmoid(spread)
    lifted_f = spread * gate
    grad_spread = back_spread * (gate + lifted_f * (1.0 - gate))
    gpool[...] = dot_nn(window_hot, grad_spread.astype(BF16))[:24]
    gpool_copies = pool_exchange(gpool, gpool_in, 1)
    lifted = lifted_f.astype(BF16)

    chunks = []
    if inside:
        bufs, ins, bias_buf, bias_in, sc_send, sc_recv, bias_send, bias_recv = (
            scatter[:6],
            scatter[6 : 6 + 6 * depth],
            *scatter[6 + 6 * depth :],
        )
        orders = [(0, 1, 2, 3), (0, 2, 1, 3), (0, 1, 2, 3), (0, 1, 2, 3), (0, 2, 1, 3), (0, 1, 2, 3)]
        bits = [lax.rem(me // (1 << level), 2) for level in range(depth)]

        def place(order, shard):
            return sum(((shard >> bit) & 1) << (depth - 1 - i) for i, bit in enumerate(order))

        pending = {}
        bases = [[0] * (depth + 1) for _ in range(6)]

        def send_half(c, level):
            order, half = orders[c], n >> (level + 1)
            bit = bits[order[level]]
            base = bases[c][level]
            bases[c][level + 1] = base + bit * half
            copy = remote(
                bufs[c].at[pl.ds(base + (1 - bit) * half, half)],
                ins[c * depth + level],
                sc_send.at[c, level],
                sc_recv.at[c, level],
                me + (1 - 2 * bit) * (1 << order[level]),
            )
            copy.start()
            pending[c, level] = copy

        def advance(c, level):
            pending[c, level].wait_recv()
            arrived = ins[c * depth + level]
            base = bases[c][level + 1]
            if level == depth - 1:
                return bufs[c][base].astype(F32) + arrived[0].astype(F32)
            half = n >> (level + 2)
            bit = bits[orders[c][level + 1]]

            def add(offset):
                target = pl.ds(base + offset, half)
                mine = bufs[c][target].astype(F32) + arrived[pl.ds(offset, half)].astype(F32)
                bufs[c][target] = mine.astype(BF16)

            add((1 - bit) * half)
            send_half(c, level + 1)
            add(bit * half)
            return None

        def store(c, value):
            rows = value.shape[0] // n
            for shard in range(n):
                bufs[c][place(orders[c], shard)] = value[
                    shard * rows : (shard + 1) * rows
                ].astype(BF16)

    grad_back = dot_tn(lifted, grad_top)
    if inside:
        store(0, grad_back)
        send_half(0, 0)
    else:
        g_back[...] = grad_back
    top = mid.astype(F32) + dot_nn(lifted, w_back[...])
    fields[...] = (top * valid_f).astype(BF16)

    finish_slope(hid // 2)
    gsum = jnp.concatenate(pool_total(gpool, gpool_in, gpool_copies), axis=0) * inverse
    gsum = jnp.concatenate([gsum, zeros8], axis=0)
    upper = gsum.astype(BF16)
    lower = (gsum - upper.astype(F32)).astype(BF16)
    lifted_grad = dot_nn(node_hot, jnp.concatenate([upper, lower, tail], axis=0))
    grad_mid_f = (grad_top.astype(F32) + lifted_grad) * valid_f
    grad_mid = grad_mid_f.astype(BF16)
    if inside:
        advance(0, 0)
    grad_out_w = dot_nn(gathered_t[...], grad_mid)
    if inside:
        store(1, grad_out_w)
        send_half(1, 0)
    else:
        g_out[...] = grad_out_w

    for start in range(0, hid, wide):
        cols = slice(start, start + wide)
        back = dot_nt(grad_mid, w_out[cols, :]).astype(BF16)
        grad_pre = (dot_nn(hot[:, ext:], back) * slope[:, cols]).astype(BF16)
        sums = dot_nn(hot_t[...], grad_pre).astype(BF16)
        spread_sum[:, cols] = sums
        partial = grad_pre.astype(F32).reshape(num_edges // 8, 8, wide).sum(axis=0)
        upper_grad = dot_nn(table_t[...], sums[:ext])
        lower_grad = dot_nn(table_t[:, :num_nodes], sums[ext:])
        if inside:
            for left in range(0, wide, 128):
                bias_buf[(start + left) // 128] = partial[:, left : left + 128]
            c = 2 + start // wide
            store(c, jnp.concatenate([upper_grad, lower_grad], axis=0))
            send_half(c, 0)
            for step in (((1, 0),), ((2, 0),), ((3, 0), (0, 1)), ((4, 0),))[c - 2]:
                advance(*step)
        else:
            g_bias[:, cols] = partial
            g_in[:latent, cols] = upper_grad
            g_in[latent:, cols] = lower_grad

    def send_bias():
        copies = []
        for offset in range(1, n):
            copy = remote(
                bias_buf.at[beside(offset) * (hid // n) // 128],
                bias_in.at[offset - 1],
                bias_send.at[offset - 1],
                bias_recv.at[offset - 1],
                beside(offset),
            )
            copy.start()
            copies.append(copy)
        return copies

    halo_grad = dot_nt(spread_sum[num_nodes:ext, :], w_in[:latent, :])
    back_out[...] = halo_grad.astype(BF16)
    if inside:
        bias_copies = send_bias()
    back_copies = halo_exchange(back_out, back_in, 0, back_send, back_recv)
    if inside:
        advance(5, 0)
    local = dot_nt(spread_sum[:num_nodes, :], w_in[:latent, :])
    local = local + dot_nt(spread_sum[ext:, :], w_in[latent:, :]) + grad_mid.astype(F32)
    if inside:
        advance(0, 2)
        advance(1, 1)
        advance(2, 1)
        g_back[...] = advance(0, depth - 1)
    halo_wait(back_copies, True)
    owner_hot = hot_rows(send_rows, num_nodes)
    local = local + dot_nn(owner_hot, back_in[...])
    grad_nodes[...] = (local * valid_f).astype(BF16)
    if inside:
        line = bias_buf[me * (hid // n) // 128]
        for i, copy in enumerate(bias_copies):
            copy.wait_recv()
            line = line + bias_in[i]
        g_bias[...] = line
        for step in ((3, 1), (4, 1), (1, 2), (5, 1), (2, 2), (3, 2), (4, 2), (5, 2)):
            advance(*step)
        g_out[...] = advance(1, depth - 1)
        for i in range(4):
            g_in[:, i * wide : (i + 1) * wide] = advance(2 + i, depth - 1)
        for copy in pending.values():
            copy.wait_send()
        for copy in bias_copies:
            copy.wait_send()
    halo_wait(halo_copies, False)
    halo_wait(back_copies, False)
    for copy in pool_copies + gpool_copies:
        copy.wait_send()


def finish(g_bias, *refs):
    wholes, results, bias, sem = refs[:5], refs[5:10], refs[10], refs[11]
    copies = [
        pltpu.make_async_copy(source, target, sem.at[i])
        for i, (source, target) in enumerate(zip(wholes, results))
    ]
    for copy in copies:
        copy.start()
    line = jnp.sum(g_bias[...], axis=0, keepdims=True)
    width = bias.shape[0]
    place = lax.rem(lax.axis_index("dom") * width, 128) // width
    mine = line[:, :width]
    for i in range(1, 128 // width):
        mine = jnp.where(place == i, line[:, i * width : (i + 1) * width], mine)
    bias[...] = mine.reshape(width)
    for copy in copies:
        copy.wait()


def body(
    nodes, node_count, edge_src, edge_dst, edge_count, send_list, assign,
    w_in, b_in, w_out, w_back, grad_out,
):
    num_nodes, latent = nodes.shape
    num_edges = edge_src.shape[0]
    hid = b_in.shape[0]
    n = lax.axis_size("dom")
    halo = send_list.shape[1] * send_list.shape[2]
    ext = num_nodes + halo
    inside = n == 16 and scatters_inside(n, (2 * latent, hid, latent))
    depth = n.bit_length() - 1
    share = n if inside else 1
    vmem = pl.BlockSpec(memory_space=pltpu.VMEM)
    smem = pl.BlockSpec(memory_space=pltpu.SMEM)
    anywhere = pl.BlockSpec(memory_space=pl.ANY)
    dma = pltpu.SemaphoreType.DMA
    scratch = [
        pltpu.VMEM(w_in.shape, BF16),
        pltpu.VMEM(w_out.shape, BF16),
        pltpu.VMEM(w_back.shape, BF16),
        pltpu.VMEM(nodes.shape, BF16),
        pltpu.VMEM((1, num_edges), I32),
        pltpu.VMEM((1, num_edges), I32),
        pltpu.VMEM(send_list.shape, I32),
        pltpu.VMEM((1, num_nodes), I32),
        pltpu.VMEM((1, hid), F32),
        pltpu.VMEM(grad_out.shape, BF16),
        dma((10,)),
        pltpu.VMEM((ext, latent), BF16),
        pltpu.VMEM((halo, latent), BF16),
        dma((8,)),
        dma((8,)),
        pltpu.VMEM((latent, ext), BF16),
        pltpu.VMEM((hid, num_nodes), BF16),
        pltpu.VMEM((num_edges, ext + num_nodes), BF16),
        pltpu.VMEM((ext + num_nodes, num_edges), BF16),
        pltpu.VMEM((ext + num_nodes, hid), BF16),
        pltpu.VMEM((num_edges, hid), F32),
        pltpu.VMEM((num_nodes, hid), BF16),
        pltpu.VMEM((ext + num_nodes, hid), BF16),
        pltpu.VMEM((24, latent + 128), F32),
        pltpu.VMEM((4, 16, latent + 128), F32),
        pltpu.VMEM((24, latent), F32),
        pltpu.VMEM((4, 16, latent), F32),
        dma((2, 4)),
        dma((2, 4)),
        pltpu.VMEM((halo, latent), BF16),
        pltpu.VMEM((halo, latent), BF16),
        dma((8,)),
        dma((8,)),
    ]
    if inside:
        sizes = ((latent, latent), (hid, latent)) + ((2 * latent, 256),) * 4
        scratch += [pltpu.VMEM((n, rows // n, cols), BF16) for rows, cols in sizes]
        scratch += [
            pltpu.VMEM((n >> (level + 1), rows // n, cols), BF16)
            for rows, cols in sizes
            for level in range(depth)
        ]
        scratch += [
            pltpu.VMEM((hid // 128, 8, 128), F32),
            pltpu.VMEM((n - 1, 8, 128), F32),
            dma((6, depth)),
            dma((6, depth)),
            dma((n - 1,)),
            dma((n - 1,)),
        ]
    shapes = (
        jax.ShapeDtypeStruct((num_nodes, latent), BF16),
        jax.ShapeDtypeStruct((num_nodes, latent), BF16),
        jax.ShapeDtypeStruct((2 * latent // share, hid), F32),
        jax.ShapeDtypeStruct((8, 128 if inside else hid), F32),
        jax.ShapeDtypeStruct((hid // share, latent), F32),
        jax.ShapeDtypeStruct((latent // share, latent), F32),
    )
    fields, grad_nodes, g_in, g_bias, g_out, g_back = pl.pallas_call(
        functools.partial(kernel, n, inside),
        out_shape=shapes,
        in_specs=[anywhere, smem, anywhere, anywhere, smem] + [anywhere] * 7,
        out_specs=[vmem] * 6,
        scratch_shapes=scratch,
        compiler_params=pltpu.CompilerParams(
            collective_id=0, has_side_effects=True, vmem_limit_bytes=56 * 1024 * 1024
        ),
        name="mesh_step",
    )(
        nodes,
        node_count,
        edge_src.reshape(1, -1),
        edge_dst.reshape(1, -1),
        edge_count,
        send_list,
        assign.reshape(1, -1),
        w_in,
        b_in.reshape(1, -1),
        w_out,
        w_back,
        grad_out,
    )
    if inside:
        wholes = (fields, grad_nodes, g_in, g_out, g_back)
        fields, grad_nodes, g_in, g_out, g_back, bias = pl.pallas_call(
            finish,
            out_shape=[jax.ShapeDtypeStruct(whole.shape, whole.dtype) for whole in wholes]
            + [jax.ShapeDtypeStruct((hid // n,), F32)],
            in_specs=[vmem] * 6,
            out_specs=[anywhere] * 5 + [vmem],
            scratch_shapes=[dma((5,))],
            name="place_results",
        )(g_bias, *wholes)
        return fields, grad_nodes, g_in, bias, g_out, g_back
    bias = jnp.sum(g_bias, axis=0)
    summed = [
        lax.psum_scatter(value, "dom", scatter_dimension=0, tiled=True)
        for value in (g_in, bias, g_out, g_back)
    ]
    return (fields, grad_nodes, *summed)


def solution(mesh):
    rows = P(("parts", "dom"), None)
    line = P(("parts", "dom"))
    return jax.shard_map(
        body,
        mesh=mesh,
        in_specs=(
            rows, line, line, line, line, P(("parts", "dom"), None, None), line,
            P(), P(), P(), P(), rows,
        ),
        out_specs=(rows, rows, rows, line, rows, rows),
        check_vma=False,
    )
```
